512 devices in a mesh: pop: 8 (over z_hi, x), dp: 4 (over y), tensor: 16 (over z_lo, core).
Axes of the slice: x: 4, y: 4, z: 16 (z_hi: 2, z_lo: 8; z = z_hi * 8 + z_lo), core: 2. Of those that a mesh axis runs over, the one named last changes fastest.
Arguments:
- ranking: int32 [8], replicated, may hold values from 0 to 7, each once
- factor_index: int32 [8, 2, 20], replicated, may hold values from 0 to 2
- weights: bfloat16 [8, 2, 2560, 5120], P('pop', None, 'tensor', 'dp'), may hold values from -0.078125 to 0.078125
- first_moment: float32 [8, 2, 2560, 5120], P('pop', None, 'tensor', 'dp'), may hold values from -12 to 12
- second_moment: float32 [8, 2, 2560, 5120], P('pop', None, 'tensor', 'dp'), may hold values from 1 to 40
- activations: bfloat16 [8, 1024, 5120], P('pop', 'dp', 'tensor')
- cotangent: bfloat16 [8, 1024, 5120], P('pop', 'dp', 'tensor'), may hold values from -6 to 6
Outputs:
- update: bfloat16 [8, 2, 2560, 5120], P('pop', None, 'tensor', 'dp')
The draws below stay inside these ranges and needn't reach their ends.
Inputs may be any that keep to these rules, and one draw needn't show every extreme that they name: `ranking`: a permutation of the members, best first.
All inputs are finite; a program needn't handle non-finite values.
Results may differ from the reference program's by a relative error of at most 0.012.
Values may be sent and summed in bfloat16 or wider, within the bound.
A program may use at most 128 MiB of HBM per device.

```python
import math
import jax
import jax.numpy as jnp
from jax import lax

D = 5120
HEADS = 20
HEAD_SIZE = 128
HD = 2560
TOK_DEV = 256
TOKENS = 1024
MEMBERS = 8
N_DP = 4


def draw_activations(key, part):
    key = jax.random.fold_in(key, 11)
    key_rows, key_cols, key_base = jax.random.split(key, 3)
    row_scale = jnp.exp(jax.random.uniform(key_rows, (MEMBERS, TOKENS, 1), jnp.float32) * 2.302585)
    col_scale = jnp.exp(jax.random.uniform(key_cols, (MEMBERS, 1, D), jnp.float32) * 2.302585)
    base = jax.random.normal(key_base, (MEMBERS, TOKENS, D), jnp.float32)
    return (0.3 * base * row_scale * col_scale).astype(jnp.bfloat16)


def place_ends(values, key, low, largest):
    spot = [jax.random.randint(jax.random.fold_in(key, axis), (), 0, length) for axis, length in enumerate(values.shape)]
    longest = values.shape.index(max(values.shape))
    neighbour = spot[:longest] + [(spot[longest] + 1) % values.shape[longest]] + spot[longest + 1:]
    return values.at[tuple(spot)].set(low).at[tuple(neighbour)].set(largest)


def block_scale(key, dims, pieces, least, high):
    level = 1.0
    for axis_at, shards_of in pieces:
        draws = jax.random.uniform(jax.random.fold_in(jax.random.fold_in(key, 6), axis_at), (shards_of,), jnp.float32, least / len(pieces), high / len(pieces))
        level = level * jnp.repeat(jnp.exp(draws), dims[axis_at] // shards_of).reshape((-1,) + (1,) * (len(dims) - 1 - axis_at))
    return level


def gaussian(own_key, shape, width, most, cuts=(), held_as=jnp.bfloat16):
    loudness = block_scale(own_key, shape, cuts, -0.22, 0.18) if cuts else 1.0
    values = jax.random.normal(own_key, shape, jnp.float32) * width * loudness
    return jnp.minimum(jnp.maximum(values, -most), most).astype(held_as)


def setup_inputs(seed: int = 0) -> dict:
    streams_of = jax.random.split(jax.random.key(seed), 8)
    ranking = jax.random.permutation(streams_of[0], MEMBERS).astype(jnp.int32)
    factor_index = place_ends(jax.random.randint(streams_of[1], (MEMBERS, 2, HEADS), 0, 3), jax.random.fold_in(streams_of[1], 1), 0, 2).astype(jnp.int32)
    weights = gaussian(streams_of[2], (MEMBERS, 2, HD, D), D ** -0.5, 0.078125, ((0, 8), (2, 16), (3, 4)))
    first_moment = gaussian(streams_of[3], (MEMBERS, 2, HD, D), 2.0, 12.0, ((0, 8), (2, 16), (3, 4)), jnp.float32)
    second_moment = jnp.clip(jnp.exp(math.log(40.0) - 3.6888795 * jax.random.uniform(streams_of[4], (MEMBERS, 2, HD, D), jnp.float32) ** block_scale(streams_of[4], (MEMBERS, 2, HD, D), ((0, 8), (2, 16), (3, 4)), -0.2, 0.2)), 1.0, 40.0)
    activations = draw_activations(jax.random.fold_in(streams_of[7], 71), 0)
    cotangent = gaussian(streams_of[6], (MEMBERS, TOKENS, D), 1.0, 6.0, ((0, 8), (1, 4), (2, 16)))
    return dict(ranking=ranking, factor_index=factor_index, weights=weights, first_moment=first_moment, second_moment=second_moment, activations=activations, cotangent=cotangent)


rate_levels = (0.8, 1.0, 1.25)
beta_one = 0.9
beta_two = 0.95
adam_step = 10
decay = 0.1
epsilon = 1e-08

def member_step(packed):
    weights, first_moment, second_moment, activations, cotangent, factor = packed
    wide = activations.astype(jnp.float32)
    normed = (wide * lax.rsqrt(lax.optimization_barrier(jnp.mean(wide * wide, axis=1, keepdims=True)) + 1e-05)).astype(jnp.bfloat16)
    value_rows = jnp.dot(normed, weights[0].T, preferred_element_type=jnp.float32).astype(jnp.bfloat16)
    value_grad = jnp.dot(cotangent, weights[1].T, preferred_element_type=jnp.float32).astype(jnp.bfloat16)
    normed_blocks = normed.reshape(N_DP, TOK_DEV, D).astype(jnp.float32)
    grad_blocks = cotangent.reshape(N_DP, TOK_DEV, D).astype(jnp.float32)
    value_blocks = value_rows.reshape(N_DP, TOK_DEV, HD).astype(jnp.float32)
    vgrad_blocks = value_grad.reshape(N_DP, TOK_DEV, HD).astype(jnp.float32)
    first_terms = lax.optimization_barrier(jnp.einsum('bte,btd->bed', vgrad_blocks, normed_blocks).astype(jnp.bfloat16))
    second_terms = lax.optimization_barrier(jnp.einsum('bte,btd->bed', value_blocks, grad_blocks).astype(jnp.bfloat16))
    gradient = jnp.stack([lax.optimization_barrier(jnp.sum(first_terms.astype(jnp.float32), axis=0)), lax.optimization_barrier(jnp.sum(second_terms.astype(jnp.float32), axis=0))])
    new_first = beta_one * first_moment + (1.0 - beta_one) * gradient
    new_second = beta_two * second_moment + (1.0 - beta_two) * gradient * gradient
    first_hat = new_first / (1.0 - beta_one ** adam_step)
    second_hat = new_second / (1.0 - beta_two ** adam_step)
    factor_rows = jnp.repeat(factor, HEAD_SIZE, axis=1)[:, :, None]
    step_value = -factor_rows * (first_hat / (jnp.sqrt(second_hat) + epsilon) + decay * weights.astype(jnp.float32))
    return step_value.astype(jnp.bfloat16)

def reference(ranking, factor_index, weights, first_moment, second_moment, activations, cotangent):
    members = ranking.shape[0]
    half_count = members // 2
    source = jnp.zeros((members,), jnp.int32).at[ranking].set(jnp.concatenate([ranking[:half_count], ranking[:half_count]]).astype(jnp.int32))
    placed = jnp.zeros((members,), jnp.int32).at[ranking].set(jnp.arange(members, dtype=jnp.int32))
    is_loser = placed >= half_count
    levels = jnp.array(rate_levels, jnp.float32)
    chosen = lax.optimization_barrier(jnp.sum(jnp.where(factor_index[..., None] == jnp.arange(3, dtype=jnp.int32), levels, jnp.float32(0.0)), axis=-1))
    factor = jnp.where(is_loser[:, None, None], chosen, jnp.float32(1.0))
    copied_weights = jnp.take(weights, source, axis=0)
    copied_first = jnp.take(first_moment, source, axis=0)
    copied_second = jnp.take(second_moment, source, axis=0)
    return lax.map(member_step, (copied_weights, copied_first, copied_second, activations, cotangent, factor))
```

```python
import functools

import jax
import jax.numpy as jnp
from jax import lax
from jax.experimental import pallas as pl
from jax.experimental.pallas import tpu as pltpu
from jax.sharding import PartitionSpec as P

HEAD_SIZE = 128
HALF = 128
SHIFT = 1.0 / 1024.0

rate_levels = (0.8, 1.0, 1.25)
beta_one = 0.9
beta_two = 0.95
adam_step = 10
decay = 0.1
epsilon = 1e-08
MESH = pl.DeviceIdType.MESH


def kernel(
    n_dp, n_tensor,
    xt_ref, w_ref, m1_ref, m2_ref, fac_ref,
    own_ref, par_ref,
    line, feat, psend, precv, arows, grad,
    xt_sem, left_sem, right_sem, line_sem, loc_sem, y_send, y_recv, sib_send, sib_recv,
    rs_send, rs_recv, ag_send, ag_recv,
):
    j = lax.axis_index("dp")
    i = lax.axis_index("tensor")
    chips = n_tensor // 2
    c = i // 2
    core = i % 2
    sib = c * 2 + 1 - core
    per_row = chips // n_dp
    rounds = xt_ref.shape[0]
    block = xt_ref.shape[2]
    rows = w_ref.shape[1]
    cols = w_ref.shape[2]
    width = n_dp * cols

    def to(dst, src, send, recv, **where):
        return pltpu.make_async_remote_copy(
            src_ref=src, dst_ref=dst, send_sem=send, recv_sem=recv,
            device_id=where, device_id_type=MESH,
        )

    barrier = pltpu.get_barrier_semaphore()
    pl.semaphore_signal(barrier, inc=1, device_id={"tensor": sib}, device_id_type=MESH)
    for k in range(1, n_dp):
        pl.semaphore_signal(
            barrier, inc=1, device_id={"dp": (j + k) % n_dp}, device_id_type=MESH
        )

    @pl.when(c > 0)
    def _():
        pl.semaphore_signal(barrier, inc=1, device_id={"tensor": i - 2}, device_id_type=MESH)

    @pl.when(c < chips - 1)
    def _():
        pl.semaphore_signal(barrier, inc=1, device_id={"tensor": i + 2}, device_id_type=MESH)

    inner = (c > 0) & (c < chips - 1)

    @pl.when(inner)
    def _():
        pl.semaphore_wait(barrier, n_dp + 2)

    @pl.when(jnp.logical_not(inner))
    def _():
        pl.semaphore_wait(barrier, n_dp + 1)

    def place(r, row, q):
        return feat.at[r, row, :, pl.ds(((q % per_row) * 2 + core) * block, block), :]

    def sib_place(r, row, q):
        return feat.at[r, row, :, pl.ds(((q % per_row) * 2 + 1 - core) * block, block), :]

    def go_right(r, q):
        return to(line.at[r, q], line.at[r, q], right_sem.at[r, q], line_sem.at[r, q], tensor=i + 2)

    def go_left(r, q):
        return to(line.at[r, q], line.at[r, q], left_sem.at[r, q], line_sem.at[r, q], tensor=i - 2)

    def keep(r, q):
        return pltpu.make_async_copy(line.at[r, q], place(r, j, q), loc_sem.at[r, q % per_row])

    def keep_sib(r, q):
        return to(
            place(r, j, q), line.at[r, q],
            sib_send.at[r, j, q % per_row], sib_recv.at[r, j, q % per_row], tensor=sib,
        )

    def across(r, q):
        return to(
            place(r, j, q), line.at[r, q],
            y_send.at[r, q], y_recv.at[r, j, q % per_row], dp=q // per_row,
        )

    def arrive(r, row, q):
        return to(
            place(r, row, q), place(r, row, q),
            y_send.at[r, q], y_recv.at[r, row, q % per_row], dp=row,
        )

    def pass_sib(r, row, q):
        return to(
            place(r, row, q), place(r, row, q),
            sib_send.at[r, row, q % per_row], sib_recv.at[r, row, q % per_row], tensor=sib,
        )

    def from_sib(r, row, q):
        return to(
            sib_place(r, row, q), sib_place(r, row, q),
            sib_send.at[r, row, q % per_row], sib_recv.at[r, row, q % per_row], tensor=sib,
        )

    def deliver(r, q):
        @pl.when(q // per_row == j)
        def _():
            keep_sib(r, q).start()
            keep(r, q).start()

        @pl.when(q // per_row != j)
        def _():
            across(r, q).start()

    def own_sends(r):
        @pl.when(c < chips - 1)
        def _():
            go_right(r, c).start()

        @pl.when(c > 0)
        def _():
            go_left(r, c).start()

        deliver(r, c)

    def collect(r, q):
        @pl.when(q // per_row == j)
        def _():
            for k in range(1, n_dp):
                row = (j + k) % n_dp
                arrive(r, row, q).wait_recv()
                pass_sib(r, row, q).start()

    def line_step(r, s):
        @pl.when((s >= 1) & (c - s >= 0))
        def _():
            q = c - s
            go_right(r, q).wait_recv()

            @pl.when(c < chips - 1)
            def _():
                go_right(r, q).start()

            deliver(r, q)

        @pl.when((s >= 1) & (c + s < chips))
        def _():
            q = c + s
            go_left(r, q).wait_recv()

            @pl.when(c > 0)
            def _():
                go_left(r, q).start()

            deliver(r, q)

        @pl.when(s == 1)
        def _():
            collect(r, c)

        @pl.when((s >= 2) & (c - s + 1 >= 0))
        def _():
            collect(r, c - s + 1)

        @pl.when((s >= 2) & (c + s - 1 < chips))
        def _():
            collect(r, c + s - 1)

    def rs_copy(r, peer):
        return to(
            precv.at[r, j], psend.at[r, peer], rs_send.at[r, peer], rs_recv.at[r, j], dp=peer
        )

    def rs_arrive(r, peer):
        return to(
            precv.at[r, peer], psend.at[r, peer], rs_send.at[r, peer], rs_recv.at[r, peer], dp=peer
        )

    def ag_copy(r, peer):
        return to(
            arows.at[r, j], arows.at[r, j], ag_send.at[r, peer], ag_recv.at[r, j], dp=peer
        )

    def ag_arrive(r, peer):
        return to(
            arows.at[r, peer], arows.at[r, peer], ag_send.at[r, peer], ag_recv.at[r, peer], dp=peer
        )

    def joined(r, a):
        return jnp.concatenate([feat[r, row, a] for row in range(n_dp)], axis=1)

    def products(r):
        for row in range(n_dp):
            for k in range(per_row):
                from_sib(r, row, k).wait_recv()
        for k in range(per_row):
            keep(r, j * per_row + k).wait()
        for a in range(2):
            part = jnp.dot(w_ref[a], joined(r, a), preferred_element_type=jnp.float32)
            for row in range(n_dp):
                psend[r, row, a * rows:(a + 1) * rows, :] = part[
                    :, row * HALF:(row + 1) * HALF
                ].astype(jnp.bfloat16)
        for row in range(n_dp):
            wide = feat[r, row, 0].astype(jnp.float32)
            total = jnp.sum(wide * wide, axis=0, keepdims=True) * SHIFT
            high = total.astype(jnp.bfloat16)
            low = jnp.where(total < 1e37, total - high.astype(jnp.float32), 0.0)
            psend[r, row, 2 * rows:2 * rows + 16, :] = jnp.concatenate(
                [high.astype(jnp.float32), low, jnp.zeros((14, HALF), jnp.float32)], axis=0
            ).astype(jnp.bfloat16)
        for k in range(1, n_dp):
            rs_copy(r, (j + k) % n_dp).start()

    def reduce(r):
        acc = psend[r, j].astype(jnp.float32)
        for k in range(1, n_dp):
            row = (j + k) % n_dp
            rs_arrive(r, row).wait_recv()
            acc = acc + precv[r, row].astype(jnp.float32)
        total = acc[2 * rows:2 * rows + 1] + acc[2 * rows + 1:2 * rows + 2]
        scale = lax.rsqrt(total * (1.0 / (SHIFT * width)) + 1e-05)
        live = scale > 0.0
        arows[r, j, 0] = jnp.where(live, acc[rows:2 * rows] * scale, 0.0).astype(jnp.bfloat16)
        arows[r, j, 1] = jnp.where(live, acc[:rows] * scale, 0.0).astype(jnp.bfloat16)
        for k in range(1, n_dp):
            ag_copy(r, (j + k) % n_dp).start()

    def gradients(r):
        for k in range(1, n_dp):
            ag_arrive(r, (j + k) % n_dp).wait_recv()
        for a in range(2):
            mine = jnp.concatenate([arows[r, row, a] for row in range(n_dp)], axis=1)
            part = lax.dot_general(
                mine, joined(r, a), (((1,), (1,)), ((), ())), preferred_element_type=jnp.float32
            )
            grad[a] = jnp.where(r % 2 == 0, part, grad[a] + part)

    def adam(a, tile):
        here = pl.ds(pl.multiple_of(tile * 128, 128), 128)
        gradient = grad[a, :, here]
        new_first = beta_one * m1_ref[a, :, here] + (1.0 - beta_one) * gradient
        new_second = beta_two * m2_ref[a, :, here] + (1.0 - beta_two) * gradient * gradient
        first_hat = new_first / (1.0 - beta_one**adam_step)
        second_hat = new_second / (1.0 - beta_two**adam_step)
        return here, (
            first_hat / (jnp.sqrt(second_hat) + epsilon)
            + decay * w_ref[a, :, here].astype(jnp.float32)
        )

    tiles = cols // 128

    def update_own():
        for a in range(2):
            def one(tile, carry):
                here, step = adam(a, tile)
                own_ref[a, :, here] = (-step).astype(jnp.bfloat16)
                return carry

            lax.fori_loop(0, tiles, one, 0)

    def update_partner():
        half = rows // 2
        for a in range(2):
            factor = -fac_ref[a]

            def one(tile, carry):
                _, step = adam(a, tile)
                step = (factor * step).astype(jnp.bfloat16)
                par_ref[a * 2 * tiles + tile] = step[:half]
                par_ref[(a * 2 + 1) * tiles + tile] = step[half:]
                return carry

            lax.fori_loop(0, tiles, one, 0)

    for r in range(rounds):
        pltpu.make_async_copy(xt_ref.at[r], line.at[r, c], xt_sem.at[r]).start()
    for r in range(rounds):
        pltpu.make_async_copy(xt_ref.at[r], line.at[r, c], xt_sem.at[r]).wait()
    own_sends(0)

    def turn(r, carry):
        def one(s, carry):
            @pl.when(r < rounds)
            def _():
                line_step(r, s)

            @pl.when((r + 1 < rounds) & (s == chips // 2))
            def _():
                own_sends(r + 1)

            @pl.when((r > 0) & (s == 2))
            def _():
                products(r - 1)

            @pl.when((r > 0) & (s == chips // 2))
            def _():
                reduce(r - 1)

            @pl.when((r > 0) & (s == chips - 2))
            def _():
                gradients(r - 1)

            return carry

        lax.fori_loop(1, chips + 1, one, 0)

        @pl.when(r == 2)
        def _():
            update_own()

        return carry

    lax.fori_loop(0, rounds + 1, turn, 0)
    update_partner()

    def drain(r, carry):
        def one(q, carry):
            @pl.when((q <= c) & (c < chips - 1))
            def _():
                go_right(r, q).wait_send()

            @pl.when((q >= c) & (c > 0))
            def _():
                go_left(r, q).wait_send()

            @pl.when(q // per_row != j)
            def _():
                across(r, q).wait_send()

            return carry

        lax.fori_loop(0, chips, one, 0)
        for row in range(n_dp):
            for k in range(per_row):
                pass_sib(r, row, k).wait_send()
        for k in range(1, n_dp):
            peer = (j + k) % n_dp
            rs_copy(r, peer).wait_send()
            ag_copy(r, peer).wait_send()
        return carry

    lax.fori_loop(0, rounds, drain, 0)


def exploit_step(xt, weights, first_moment, second_moment, factor):
    n_dp, n_tensor = lax.axis_size("dp"), lax.axis_size("tensor")
    rounds, _, block, _ = xt.shape
    _, rows, cols = weights.shape
    chips = n_tensor // 2
    per_row = chips // n_dp
    dma = pltpu.SemaphoreType.DMA
    vmem = pl.BlockSpec(memory_space=pltpu.VMEM)
    half_tiles = 2 * 2 * (cols // 128)
    flops = rounds * 2 * 2 * 2 * rows * cols * n_dp * HALF
    return pl.pallas_call(
        functools.partial(kernel, n_dp, n_tensor),
        out_shape=(
            jax.ShapeDtypeStruct((2, rows, cols), jnp.bfloat16),
            jax.ShapeDtypeStruct((half_tiles, rows // 2, 128), jnp.bfloat16),
        ),
        in_specs=[vmem] * 5,
        out_specs=(vmem, vmem),
        scratch_shapes=[
            pltpu.VMEM((rounds, chips, 2, block, HALF), jnp.bfloat16),
            pltpu.VMEM((rounds, n_dp, 2, cols, HALF), jnp.bfloat16),
            pltpu.VMEM((rounds, n_dp, 2 * rows + 16, HALF), jnp.bfloat16),
            pltpu.VMEM((rounds, n_dp, 2 * rows + 16, HALF), jnp.bfloat16),
            pltpu.VMEM((rounds, n_dp, 2, rows, HALF), jnp.bfloat16),
            pltpu.VMEM((2, rows, cols), jnp.float32),
            dma((rounds,)),
            dma((rounds, chips)),
            dma((rounds, chips)),
            dma((rounds, chips)),
            dma((rounds, per_row)),
            dma((rounds, chips)),
            dma((rounds, n_dp, per_row)),
            dma((rounds, n_dp, per_row)),
            dma((rounds, n_dp, per_row)),
            dma((rounds, n_dp)),
            dma((rounds, n_dp)),
            dma((rounds, n_dp)),
            dma((rounds, n_dp)),
        ],
        compiler_params=pltpu.CompilerParams(
            collective_id=0, has_side_effects=True, vmem_limit_bytes=56 * 1024 * 1024
        ),
        cost_estimate=pl.CostEstimate(
            flops=flops, bytes_accessed=8 * rows * cols * 4, transcendentals=0
        ),
        name="gather_and_step",
    )(xt, weights, first_moment, second_moment, factor)


def swap(pieces, chosen):
    arrived = lax.all_to_all(pieces, "pop", split_axis=0, concat_axis=0, tiled=True)
    picked = jnp.take(arrived, chosen, axis=0)
    return lax.all_to_all(picked, "pop", split_axis=0, concat_axis=0, tiled=True)


def per_device(ranking, factor_index, weights, first_moment, second_moment, activations, cotangent):
    members = lax.axis_size("pop")
    half_count = members // 2
    member = lax.axis_index("pop")
    winners, losers = ranking[:half_count], ranking[half_count:]
    partner = (
        jnp.zeros((members,), jnp.int32).at[winners].set(losers).at[losers].set(winners)
    )
    placed = jnp.zeros((members,), jnp.int32).at[ranking].set(jnp.arange(members, dtype=jnp.int32))
    is_loser = jnp.take(placed, member) >= half_count
    levels = jnp.array(rate_levels, jnp.float32)
    partner_index = jnp.take(factor_index, jnp.take(partner, member), axis=0)
    chosen = jnp.sum(
        jnp.where(partner_index[..., None] == jnp.arange(3, dtype=jnp.int32), levels, 0.0), axis=-1
    )
    row_count = weights.shape[2]
    head_count = factor_index.shape[2]
    global_rows = lax.axis_index("tensor") * row_count + jnp.arange(row_count, dtype=jnp.int32)
    row_heads = global_rows // HEAD_SIZE
    onehot = (row_heads[:, None] == jnp.arange(head_count, dtype=jnp.int32)[None, :]).astype(
        jnp.float32
    )
    row_factor = jnp.sum(chosen[:, None, :] * onehot[None, :, :], axis=2)

    tokens, block = activations.shape[1:]
    both = jnp.stack([activations[0], cotangent[0]])
    own = both.reshape(2, 2, HALF, block).transpose(1, 0, 3, 2)
    other = swap(own.reshape(members, -1, HALF), partner).reshape(own.shape)
    own_step, partner_step = exploit_step(
        jnp.concatenate([own, other]),
        weights[0], first_moment[0], second_moment[0], row_factor[:, :, None],
    )
    rows, cols = weights.shape[2:]
    tiles = partner_step.shape[0]
    returned = swap(partner_step.reshape(members, tiles // members, rows // 2, 128), partner)
    returned = (
        returned.reshape(2, 2, cols // 128, rows // 2, 128)
        .transpose(0, 1, 3, 2, 4)
        .reshape(2, rows, cols)
    )
    return jnp.where(is_loser, returned, own_step)[None]


def solution(mesh):
    in_specs = (
        P(),
        P(),
        P("pop", None, "tensor", "dp"),
        P("pop", None, "tensor", "dp"),
        P("pop", None, "tensor", "dp"),
        P("pop", "dp", "tensor"),
        P("pop", "dp", "tensor"),
    )
    out_specs = P("pop", None, "tensor", "dp")
    return jax.shard_map(
        per_device, mesh=mesh, in_specs=in_specs, out_specs=out_specs, check_vma=False
    )
```

```python
import functools

import jax
import jax.numpy as jnp
from jax import lax
from jax.experimental import pallas as pl
from jax.experimental.pallas import tpu as pltpu
from jax.sharding import PartitionSpec as P

HEAD_SIZE = 128
HALF = 128
SHIFT = 1.0 / 1024.0

rate_levels = (0.8, 1.0, 1.25)
beta_one = 0.9
beta_two = 0.95
adam_step = 10
decay = 0.1
epsilon = 1e-08
MESH = pl.DeviceIdType.MESH


def kernel(
    n_cross, n_pop, n_dp, n_tensor,
    table, xt_ref, w_ref, m1_ref, m2_ref, fac_ref,
    out_ref,
    near0, near1, near2, far0, far1, far2, sent, back, short, w_new, m_new,
    feat, psend, precv, arows, grad,
    loc_sem, y_send, y_recv, left_sem, right_sem, line_sem, sib_send, sib_recv,
    rs_send, rs_recv, ag_send, ag_recv,
    near_send, near_recv, far_send, far_recv, back_send, back_recv,
):
    p = lax.axis_index("pop")
    n_x = n_pop // 2
    side = p // n_x
    x = p % n_x
    opposite = (p + n_x) % n_pop
    j = lax.axis_index("dp")
    i = lax.axis_index("tensor")
    chips = n_tensor // 2
    c = i // 2
    core = i % 2
    sib = c * 2 + 1 - core
    per_row = chips // n_dp
    rounds = feat.shape[0]
    block = xt_ref.shape[2]
    rows = w_ref.shape[1]
    cols = w_ref.shape[2]
    width = n_dp * cols
    steps = per_row * n_dp
    home = c // per_row
    mine = c % per_row

    def to(dst, src, send, recv, **where):
        return pltpu.make_async_remote_copy(
            src_ref=src, dst_ref=dst, send_sem=send, recv_sem=recv,
            device_id=where, device_id_type=MESH,
        )

    barrier = pltpu.get_barrier_semaphore()
    pl.semaphore_signal(barrier, inc=1, device_id={"tensor": sib}, device_id_type=MESH)
    for k in range(1, n_dp):
        pl.semaphore_signal(
            barrier, inc=1, device_id={"dp": (j + k) % n_dp}, device_id_type=MESH
        )
    for k in range(1, n_x):
        pl.semaphore_signal(
            barrier, inc=1, device_id={"pop": side * n_x + (x + k) % n_x}, device_id_type=MESH
        )
    pl.semaphore_signal(barrier, inc=1, device_id={"pop": opposite}, device_id_type=MESH)

    @pl.when(c > 0)
    def _():
        pl.semaphore_signal(barrier, inc=1, device_id={"tensor": i - 2}, device_id_type=MESH)

    @pl.when(c < chips - 1)
    def _():
        pl.semaphore_signal(barrier, inc=1, device_id={"tensor": i + 2}, device_id_type=MESH)

    inner = (c > 0) & (c < chips - 1)

    @pl.when(inner)
    def _():
        pl.semaphore_wait(barrier, n_dp + n_x + 2)

    @pl.when(jnp.logical_not(inner))
    def _():
        pl.semaphore_wait(barrier, n_dp + n_x + 1)

    def place(r, row, k, half):
        return feat.at[r, row, :, pl.ds((k * 2 + half) * block, block), :]

    def keep(r, src):
        return pltpu.make_async_copy(src, place(r, j, mine, core), loc_sem.at[r])

    def across(r, src):
        return to(place(r, j, mine, core), src, y_send.at[r], y_recv.at[r, j], dp=home)

    def arrive(r, row):
        here = place(r, row, mine, core)
        return to(here, here, y_send.at[r], y_recv.at[r, row], dp=row)

    def go_right(r, k, row):
        here = place(r, row, k, core)
        return to(here, here, right_sem.at[r, k, row], line_sem.at[r, k, row], tensor=i + 2)

    def go_left(r, k, row):
        here = place(r, row, k, core)
        return to(here, here, left_sem.at[r, k, row], line_sem.at[r, k, row], tensor=i - 2)

    def pass_sib(r, k, row):
        here = place(r, row, k, core)
        return to(here, here, sib_send.at[r, k, row], sib_recv.at[r, k, row], tensor=sib)

    def from_sib(r, k, row):
        here = place(r, row, k, 1 - core)
        return to(here, here, sib_send.at[r, k, row], sib_recv.at[r, k, row], tensor=sib)

    def spread(r):
        @pl.when(home == j)
        def _():
            keep(r, xt_ref.at[r]).start()

        @pl.when(home != j)
        def _():
            across(r, xt_ref.at[r]).start()

    def line_step(r, n):
        first = jnp.where(c <= j * per_row, 0, 1)
        k = jnp.where(n < n_dp, first, 1 - first)
        row = (j + n) % n_dp
        start = j * per_row + k

        @pl.when((start == c) & (row == j))
        def _():
            keep(r, place(r, j, mine, core)).wait()

        @pl.when((start == c) & (row != j))
        def _():
            arrive(r, row).wait_recv()

        @pl.when(start < c)
        def _():
            go_right(r, k, row).wait_recv()

        @pl.when(start > c)
        def _():
            go_left(r, k, row).wait_recv()

        @pl.when((start <= c) & (c < chips - 1))
        def _():
            go_right(r, k, row).start()

        @pl.when((start >= c) & (c > 0))
        def _():
            go_left(r, k, row).start()

        pass_sib(r, k, row).start()

    def rs_copy(r, peer):
        return to(
            precv.at[r, j], psend.at[r, peer], rs_send.at[r, peer], rs_recv.at[r, j], dp=peer
        )

    def rs_arrive(r, peer):
        return to(
            precv.at[r, peer], psend.at[r, peer], rs_send.at[r, peer], rs_recv.at[r, peer], dp=peer
        )

    def ag_copy(r, peer):
        return to(
            arows.at[r, j], arows.at[r, j], ag_send.at[r, peer], ag_recv.at[r, j], dp=peer
        )

    def ag_arrive(r, peer):
        return to(
            arows.at[r, peer], arows.at[r, peer], ag_send.at[r, peer], ag_recv.at[r, peer], dp=peer
        )

    def joined(r, a):
        return jnp.concatenate([feat[r, row, a] for row in range(n_dp)], axis=1)

    def products(r, a):
        part = jnp.dot(w_new[a], joined(r, a), preferred_element_type=jnp.float32)
        for row in range(n_dp):
            psend[r, row, a * rows:(a + 1) * rows, :] = part[
                :, row * HALF:(row + 1) * HALF
            ].astype(jnp.bfloat16)

    def first_products(r):
        for k in range(per_row):
            for row in range(n_dp):
                from_sib(r, k, row).wait_recv()
        products(r, 0)

    def second_products(r):
        products(r, 1)
        for row in range(n_dp):
            wide = feat[r, row, 0].astype(jnp.float32)
            total = jnp.sum(wide * wide, axis=0, keepdims=True) * SHIFT
            high = total.astype(jnp.bfloat16)
            low = jnp.where(total < 1e37, total - high.astype(jnp.float32), 0.0)
            psend[r, row, 2 * rows:2 * rows + 16, :] = jnp.concatenate(
                [high.astype(jnp.float32), low, jnp.zeros((14, HALF), jnp.float32)], axis=0
            ).astype(jnp.bfloat16)
        for k in range(1, n_dp):
            rs_copy(r, (j + k) % n_dp).start()

    def reduce(r):
        acc = psend[r, j].astype(jnp.float32)
        for k in range(1, n_dp):
            row = (j + k) % n_dp
            rs_arrive(r, row).wait_recv()
            acc = acc + precv[r, row].astype(jnp.float32)
        total = acc[2 * rows:2 * rows + 1] + acc[2 * rows + 1:2 * rows + 2]
        scale = lax.rsqrt(total * (1.0 / (SHIFT * width)) + 1e-05)
        live = scale > 0.0
        arows[r, j, 0] = jnp.where(live, acc[rows:2 * rows] * scale, 0.0).astype(jnp.bfloat16)
        arows[r, j, 1] = jnp.where(live, acc[:rows] * scale, 0.0).astype(jnp.bfloat16)
        for k in range(1, n_dp):
            ag_copy(r, (j + k) % n_dp).start()

    def gradients(r, a):
        mixed = jnp.concatenate([arows[r, row, a] for row in range(n_dp)], axis=1)
        part = lax.dot_general(
            mixed, joined(r, a), (((1,), (1,)), ((), ())), preferred_element_type=jnp.float32
        )
        if r == 0:
            grad[a] = part
        else:
            grad[a] = grad[a] + part

    def first_gradients(r):
        for k in range(1, n_dp):
            ag_arrive(r, (j + k) % n_dp).wait_recv()
        gradients(r, 0)

    def second_gradients(r):
        gradients(r, 1)

    def update():
        for a in range(2):
            factor = -fac_ref[a]

            def one(tile, carry):
                here = pl.ds(pl.multiple_of(tile * 128, 128), 128)
                gradient = grad[a, :, here]
                first = m_new[0, a, :, here].astype(jnp.float32)
                second = m_new[1, a, :, here].astype(jnp.float32)
                new_first = beta_one * first + (1.0 - beta_one) * gradient
                new_second = beta_two * second + (1.0 - beta_two) * gradient * gradient
                first_hat = new_first / (1.0 - beta_one**adam_step)
                second_hat = new_second / (1.0 - beta_two**adam_step)
                step = first_hat / (jnp.sqrt(second_hat) + epsilon) + decay * w_new[
                    a, :, here
                ].astype(jnp.float32)
                out_ref[a, :, here] = (factor * step).astype(jnp.bfloat16)
                return carry

            lax.fori_loop(0, cols // 128, one, 0)

    near = (near0, near1, near2)
    far = (far0, far1, far2)
    parts = n_x // 2
    size = rows // parts

    def piece(ref, q):
        return ref.at[q // parts, pl.ds(q % parts * size, size), :]

    def held(ch):
        return w_ref if ch == 0 else short.at[ch - 1]

    def new(ch):
        return w_new if ch == 0 else m_new.at[ch - 1]

    def others(f):
        for k in range(1, n_x):
            f((x + k) % n_x)

    def near_copy(ch, q):
        return to(
            near[ch].at[x], piece(held(ch), q), near_send.at[ch, q], near_recv.at[ch, x],
            pop=side * n_x + q,
        )

    def near_arrive(ch, q):
        here = near[ch].at[q]
        return to(here, here, near_send.at[ch, q], near_recv.at[ch, q], pop=side * n_x + q)

    def far_copy(ch, s):
        return to(
            far[ch].at[s], sent.at[ch, s], far_send.at[ch, s], far_recv.at[ch, s], pop=opposite
        )

    def back_copy(ch, q):
        return to(
            piece(new(ch), x), back.at[ch, q], back_send.at[ch, q], back_recv.at[ch, x],
            pop=side * n_x + q,
        )

    def back_arrive(ch, q):
        here = piece(new(ch), q)
        return to(here, here, back_send.at[ch, q], back_recv.at[ch, q], pop=side * n_x + q)

    def near_out(ch):
        others(lambda q: near_copy(ch, q).start())
        near[ch][x] = piece(held(ch), x)[...]

    def far_out(ch):
        others(lambda q: near_arrive(ch, q).wait_recv())
        for s in range(n_cross):
            sent[ch, s] = near[ch][table[s]]
            far_copy(ch, s).start()

    def back_out(ch):
        for s in range(n_cross):
            far_copy(ch, s).wait_recv()
        for q in range(n_x):
            pick = table[n_x + q]
            got = near[ch][jnp.minimum(pick, n_x - 1)]
            if n_cross:
                got = jnp.where(pick < n_x, got, far[ch][jnp.maximum(pick - n_x, 0)])
            back[ch, q] = got
        others(lambda q: back_copy(ch, q).start())
        piece(new(ch), x)[...] = back[ch, x]

    def back_in(ch):
        others(lambda q: back_arrive(ch, q).wait_recv())

    def moments(f):
        def go():
            f(1)
            f(2)

        return go

    near_out(0)
    spread(0)
    spread(1)
    for a in range(2):
        short[0, a] = m1_ref[a].astype(jnp.bfloat16)
        short[1, a] = m2_ref[a].astype(jnp.bfloat16)
    moments(near_out)()

    whole = rounds * steps
    eighth = whole // 8
    work = [(eighth, lambda: far_out(0))]
    if n_cross == 0:
        work += [
            (eighth, lambda: back_out(0)),
            (3 * eighth, moments(far_out)),
            (3 * eighth, moments(back_out)),
        ]
    elif n_cross == 1:
        work += [(5 * eighth, lambda: back_out(0)), (6 * eighth - 1, moments(far_out))]
    elif n_cross == 2:
        work += [(3 * eighth, moments(far_out)), (whole - 1, lambda: back_out(0))]
    else:
        work += [(3 * eighth, moments(far_out))]

    def turn(f, carry):
        line_step(f // steps, f % steps)
        for at, part in work:
            @pl.when(f == at)
            def _():
                part()

        return carry

    lax.fori_loop(0, whole, turn, 0)
    if n_cross > 2:
        back_out(0)
    back_in(0)
    for r in range(rounds):
        first_products(r)
        second_products(r)
    for r in range(rounds):
        reduce(r)
    first_gradients(0)
    second_gradients(0)
    if n_cross:
        moments(back_out)()
    first_gradients(1)
    second_gradients(1)
    moments(back_in)()
    update()

    def drain(r, carry):
        for k in range(per_row):
            start = j * per_row + k

            @pl.when((start <= c) & (c < chips - 1))
            def _():
                for row in range(n_dp):
                    go_right(r, k, row).wait_send()

            @pl.when((start >= c) & (c > 0))
            def _():
                for row in range(n_dp):
                    go_left(r, k, row).wait_send()

            for row in range(n_dp):
                pass_sib(r, k, row).wait_send()
        for k in range(1, n_dp):
            peer = (j + k) % n_dp
            rs_copy(r, peer).wait_send()
            ag_copy(r, peer).wait_send()

        @pl.when(home != j)
        def _():
            across(r, xt_ref.at[r]).wait_send()

        return carry

    lax.fori_loop(0, rounds, drain, 0)
    for ch in range(3):
        others(lambda q: near_copy(ch, q).wait_send())
        others(lambda q: back_copy(ch, q).wait_send())
        for s in range(n_cross):
            far_copy(ch, s).wait_send()


def exploit_step(n_cross, table, xt, weights, first_moment, second_moment, factor):
    n_pop, n_dp, n_tensor = (lax.axis_size(name) for name in ("pop", "dp", "tensor"))
    rounds = xt.shape[0]
    block = xt.shape[2]
    _, rows, cols = weights.shape
    chips = n_tensor // 2
    per_row = chips // n_dp
    n_x = n_pop // 2
    slots = max(n_cross, 1)
    dma = pltpu.SemaphoreType.DMA
    vmem = pl.BlockSpec(memory_space=pltpu.VMEM)
    bf16 = functools.partial(pltpu.VMEM, dtype=jnp.bfloat16)
    part = (4 * rows // n_pop, cols)
    flops = rounds * 2 * 2 * 2 * rows * cols * n_dp * HALF
    return pl.pallas_call(
        functools.partial(kernel, n_cross, n_pop, n_dp, n_tensor),
        out_shape=jax.ShapeDtypeStruct((2, rows, cols), jnp.bfloat16),
        in_specs=[pl.BlockSpec(memory_space=pltpu.SMEM)] + [vmem] * 5,
        out_specs=vmem,
        scratch_shapes=[bf16((n_x,) + part)] * 3
        + [bf16((slots,) + part)] * 3
        + [
            bf16((3, slots) + part),
            bf16((3, n_x) + part),
            bf16((2, 2, rows, cols)),
            bf16((2, rows, cols)),
            bf16((2, 2, rows, cols)),
            bf16((rounds, n_dp, 2, cols, HALF)),
            bf16((rounds, n_dp, 2 * rows + 16, HALF)),
            bf16((rounds, n_dp, 2 * rows + 16, HALF)),
            bf16((rounds, n_dp, 2, rows, HALF)),
            pltpu.VMEM((2, rows, cols), jnp.float32),
            dma((rounds,)),
            dma((rounds,)),
            dma((rounds, n_dp)),
            dma((rounds, per_row, n_dp)),
            dma((rounds, per_row, n_dp)),
            dma((rounds, per_row, n_dp)),
            dma((rounds, per_row, n_dp)),
            dma((rounds, per_row, n_dp)),
            dma((rounds, n_dp)),
            dma((rounds, n_dp)),
            dma((rounds, n_dp)),
            dma((rounds, n_dp)),
            dma((3, n_x)),
            dma((3, n_x)),
            dma((3, slots)),
            dma((3, slots)),
            dma((3, n_x)),
            dma((3, n_x)),
        ],
        compiler_params=pltpu.CompilerParams(
            collective_id=n_cross, has_side_effects=True, vmem_limit_bytes=56 * 1024 * 1024
        ),
        cost_estimate=pl.CostEstimate(
            flops=flops, bytes_accessed=8 * rows * cols * 4, transcendentals=0
        ),
        name=f"exploit_{n_cross}",
    )(table, xt, weights, first_moment, second_moment, factor)


def plan(ranking, side):
    members = ranking.shape[0]
    n_x = members // 2
    ids = jnp.arange(members, dtype=jnp.int32)
    placed = (ranking[:, None] == ids[None, :]).astype(jnp.int32)
    from_rank = jnp.concatenate([ranking[:n_x], ranking[:n_x]])
    source = jnp.sum(placed * from_rank[:, None], axis=0)
    loser = jnp.sum(placed[n_x:], axis=0)
    crosses = (source // n_x != ids // n_x).astype(jnp.int32)
    before = (ids[:, None] < ids[None, :]) & (ids[:, None] // n_x == ids[None, :] // n_x)
    slot = jnp.sum(crosses[:, None] * before, axis=0)
    n_cross = jnp.maximum(jnp.sum(crosses[:n_x]), jnp.sum(crosses[n_x:]))
    picks = jnp.where(crosses > 0, n_x + slot, source % n_x)
    use = (crosses > 0) & (ids // n_x != side)
    sends = jnp.sum(
        jnp.where(use[None, :] & (slot[None, :] == ids[:n_x, None]), source % n_x, 0), axis=1
    )
    mine = jnp.where(side > 0, picks[n_x:], picks[:n_x])
    return loser, n_cross, jnp.concatenate([sends, mine])


def per_device(ranking, factor_index, weights, first_moment, second_moment, activations, cotangent):
    members = lax.axis_size("pop")
    member = lax.axis_index("pop")
    loser, n_cross, table = plan(ranking, member // (members // 2))
    is_loser = jnp.sum(jnp.where(jnp.arange(members) == member, loser, 0)) > 0
    levels = jnp.array(rate_levels, jnp.float32)
    own_index = jnp.take(factor_index, member, axis=0)
    chosen = jnp.sum(
        jnp.where(own_index[..., None] == jnp.arange(3, dtype=jnp.int32), levels, 0.0), axis=-1
    )
    row_count = weights.shape[2]
    head_count = factor_index.shape[2]
    global_rows = lax.axis_index("tensor") * row_count + jnp.arange(row_count, dtype=jnp.int32)
    row_heads = global_rows // HEAD_SIZE
    onehot = (row_heads[:, None] == jnp.arange(head_count, dtype=jnp.int32)[None, :]).astype(
        jnp.float32
    )
    row_factor = jnp.sum(chosen[:, None, :] * onehot[None, :, :], axis=2)
    factor = jnp.where(is_loser, row_factor, 1.0)[:, :, None]

    block = activations.shape[2]
    both = jnp.stack([activations[0], cotangent[0]])
    own = both.reshape(2, 2, HALF, block).transpose(1, 0, 3, 2)
    step = lax.switch(
        n_cross,
        [functools.partial(exploit_step, k) for k in range(members // 2 + 1)],
        table, own, weights[0], first_moment[0], second_moment[0], factor,
    )
    return step[None]


def solution(mesh):
    in_specs = (
        P(),
        P(),
        P("pop", None, "tensor", "dp"),
        P("pop", None, "tensor", "dp"),
        P("pop", None, "tensor", "dp"),
        P("pop", "dp", "tensor"),
        P("pop", "dp", "tensor"),
    )
    out_specs = P("pop", None, "tensor", "dp")
    return jax.shard_map(
        per_device, mesh=mesh, in_specs=in_specs, out_specs=out_specs, check_vma=False
    )
```

```python
import functools

import jax
import jax.numpy as jnp
from jax import lax
from jax.experimental import pallas as pl
from jax.experimental.pallas import tpu as pltpu
from jax.sharding import PartitionSpec as P

HEAD_SIZE = 128
HALF = 128
SHIFT = 1.0 / 1024.0

rate_levels = (0.8, 1.0, 1.25)
beta_one = 0.9
beta_two = 0.95
adam_step = 10
decay = 0.1
epsilon = 1e-08
MESH = pl.DeviceIdType.MESH


def kernel(
    counts, n_pop, n_dp, n_tensor, n_heads,
    rank_ref, choice_ref, act_ref, cot_ref, w_ref, m1_ref, m2_ref,
    out_ref,
    xt_ref, wide1, wide2, near0, near1, near2, far0, far1, far2, sent, back, short, w_new, m_new,
    feat, psend, precv, arows, grad,
    loc_sem, y_send, y_recv, left_sem, right_sem, line_sem, sib_send, sib_recv,
    rs_send, rs_recv, ag_send, ag_recv,
    near_send, near_recv, far_send, far_recv, back_send, back_recv, own_sem,
):
    p = lax.axis_index("pop")
    n_x = n_pop // 2
    side = p // n_x
    x = p % n_x
    opposite = (p + n_x) % n_pop
    n_cross = max(counts)
    n_sent = jnp.where(side == 0, counts[0], counts[1])
    n_got = jnp.where(side == 0, counts[1], counts[0])
    j = lax.axis_index("dp")
    i = lax.axis_index("tensor")
    chips = n_tensor // 2
    c = i // 2
    core = i % 2
    sib = c * 2 + 1 - core
    per_row = chips // n_dp
    rounds = feat.shape[0]
    block = xt_ref.shape[2]
    rows = w_ref.shape[1]
    cols = w_ref.shape[2]
    width = n_dp * cols
    steps = per_row * n_dp
    home = c // per_row
    mine = c % per_row

    for m, (ref, wide) in enumerate(((m1_ref, wide1), (m2_ref, wide2))):
        pltpu.make_async_copy(ref, wide, own_sem.at[m]).start()

    def to(dst, src, send, recv, **where):
        return pltpu.make_async_remote_copy(
            src_ref=src, dst_ref=dst, send_sem=send, recv_sem=recv,
            device_id=where, device_id_type=MESH,
        )

    barrier = pltpu.get_barrier_semaphore()
    pl.semaphore_signal(barrier, inc=1, device_id={"tensor": sib}, device_id_type=MESH)
    for k in range(1, n_dp):
        pl.semaphore_signal(
            barrier, inc=1, device_id={"dp": (j + k) % n_dp}, device_id_type=MESH
        )
    for k in range(1, n_x):
        pl.semaphore_signal(
            barrier, inc=1, device_id={"pop": side * n_x + (x + k) % n_x}, device_id_type=MESH
        )
    pl.semaphore_signal(barrier, inc=1, device_id={"pop": opposite}, device_id_type=MESH)

    @pl.when(c > 0)
    def _():
        pl.semaphore_signal(barrier, inc=1, device_id={"tensor": i - 2}, device_id_type=MESH)

    @pl.when(c < chips - 1)
    def _():
        pl.semaphore_signal(barrier, inc=1, device_id={"tensor": i + 2}, device_id_type=MESH)

    sends = [jnp.int32(0)] * max(n_cross, 1)
    picks = [jnp.int32(q) for q in range(n_x)]
    losing = jnp.int32(0)
    arrived = [jnp.int32(0), jnp.int32(0)]
    for pair in range(n_x):
        winner, loser = rank_ref[pair], rank_ref[n_x + pair]
        w_side, l_side = lax.div(winner, n_x), lax.div(loser, n_x)
        w_x = winner - w_side * n_x
        cross = w_side != l_side
        slot = jnp.where(l_side > 0, arrived[1], arrived[0])
        arrived = [
            arrived[0] + jnp.where(cross & (l_side == 0), 1, 0),
            arrived[1] + jnp.where(cross & (l_side > 0), 1, 0),
        ]
        sends = [
            jnp.where(cross & (w_side == side) & (slot == n), w_x, old)
            for n, old in enumerate(sends)
        ]
        picks = [
            jnp.where(loser == side * n_x + q, jnp.where(cross, n_x + slot, w_x), old)
            for q, old in enumerate(picks)
        ]
        losing = jnp.where(loser == p, 1, losing)

    def levels(a, head):
        choice = choice_ref[(p * 2 + a) * n_heads + jnp.minimum(head, n_heads - 1)]
        level = jnp.where(
            choice == 0, rate_levels[0], jnp.where(choice == 1, rate_levels[1], rate_levels[2])
        )
        return jnp.where(losing > 0, level, 1.0)

    def row_factor(a):
        first_row = i * rows
        head = first_row // HEAD_SIZE
        at = lax.broadcasted_iota(jnp.int32, (rows, 128), 0) + (first_row - head * HEAD_SIZE)
        return jnp.where(
            at < HEAD_SIZE,
            levels(a, head),
            jnp.where(at < 2 * HEAD_SIZE, levels(a, head + 1), levels(a, head + 2)),
        )

    inner = (c > 0) & (c < chips - 1)

    @pl.when(inner)
    def _():
        pl.semaphore_wait(barrier, n_dp + n_x + 2)

    @pl.when(jnp.logical_not(inner))
    def _():
        pl.semaphore_wait(barrier, n_dp + n_x + 1)

    def place(r, row, k, half):
        return feat.at[r, row, :, pl.ds((k * 2 + half) * block, block), :]

    def keep(r, src):
        return pltpu.make_async_copy(src, place(r, j, mine, core), loc_sem.at[r])

    def across(r, src):
        return to(place(r, j, mine, core), src, y_send.at[r], y_recv.at[r, j], dp=home)

    def arrive(r, row):
        here = place(r, row, mine, core)
        return to(here, here, y_send.at[r], y_recv.at[r, row], dp=row)

    def place_of(r, row, k, half, a):
        return feat.at[r, row, a, pl.ds((k * 2 + half) * block, block), :]

    def go_right(r, k, row, a):
        here = place_of(r, row, k, core, a)
        at = (r, k, row, a)
        return to(here, here, right_sem.at[at], line_sem.at[at], tensor=i + 2)

    def go_left(r, k, row, a):
        here = place_of(r, row, k, core, a)
        at = (r, k, row, a)
        return to(here, here, left_sem.at[at], line_sem.at[at], tensor=i - 2)

    def pass_sib(r, k, row, a):
        here = place_of(r, row, k, core, a)
        at = (r, k, row, a)
        return to(here, here, sib_send.at[at], sib_recv.at[at], tensor=sib)

    def from_sib(r, k, row, a):
        here = place_of(r, row, k, 1 - core, a)
        at = (r, k, row, a)
        return to(here, here, sib_send.at[at], sib_recv.at[at], tensor=sib)

    def spread(r):
        @pl.when(home == j)
        def _():
            keep(r, xt_ref.at[r]).start()

        @pl.when(home != j)
        def _():
            across(r, xt_ref.at[r]).start()

    def line_step(r, n, a):
        first = jnp.where(c <= j * per_row, 0, 1)
        k = jnp.where(n < n_dp, first, 1 - first)
        row = (j + n) % n_dp
        start = j * per_row + k

        @pl.when((start == c) & (row == j) & (a == 0))
        def _():
            keep(r, place(r, j, mine, core)).wait()

        @pl.when((start == c) & (row != j) & (a == 0))
        def _():
            arrive(r, row).wait_recv()

        @pl.when(start < c)
        def _():
            go_right(r, k, row, a).wait_recv()

        @pl.when(start > c)
        def _():
            go_left(r, k, row, a).wait_recv()

        @pl.when((start <= c) & (c < chips - 1))
        def _():
            go_right(r, k, row, a).start()

        @pl.when((start >= c) & (c > 0))
        def _():
            go_left(r, k, row, a).start()

        pass_sib(r, k, row, a).start()

    def rs_copy(r, peer):
        return to(
            precv.at[r, j], psend.at[r, peer], rs_send.at[r, peer], rs_recv.at[r, j], dp=peer
        )

    def rs_arrive(r, peer):
        return to(
            precv.at[r, peer], psend.at[r, peer], rs_send.at[r, peer], rs_recv.at[r, peer], dp=peer
        )

    def ag_copy(r, peer):
        return to(
            arows.at[r, j], arows.at[r, j], ag_send.at[r, peer], ag_recv.at[r, j], dp=peer
        )

    def ag_arrive(r, peer):
        return to(
            arows.at[r, peer], arows.at[r, peer], ag_send.at[r, peer], ag_recv.at[r, peer], dp=peer
        )

    def joined(r, a):
        return jnp.concatenate([feat[r, row, a] for row in range(n_dp)], axis=1)

    def products(r, a):
        part = jnp.dot(w_new[a], joined(r, a), preferred_element_type=jnp.float32)
        for row in range(n_dp):
            psend[r, row, a * rows:(a + 1) * rows, :] = part[
                :, row * HALF:(row + 1) * HALF
            ].astype(jnp.bfloat16)

    def first_products(r):
        for k in range(per_row):
            for row in range(n_dp):
                for a in range(2):
                    from_sib(r, k, row, a).wait_recv()
        products(r, 0)

    def second_products(r):
        products(r, 1)
        for row in range(n_dp):
            wide = feat[r, row, 0].astype(jnp.float32)
            total = jnp.sum(wide * wide, axis=0, keepdims=True) * SHIFT
            high = total.astype(jnp.bfloat16)
            low = jnp.where(total < 1e37, total - high.astype(jnp.float32), 0.0)
            psend[r, row, 2 * rows:2 * rows + 16, :] = jnp.concatenate(
                [high.astype(jnp.float32), low, jnp.zeros((14, HALF), jnp.float32)], axis=0
            ).astype(jnp.bfloat16)
        for k in range(1, n_dp):
            rs_copy(r, (j + k) % n_dp).start()

    def reduce(r):
        acc = psend[r, j].astype(jnp.float32)
        for k in range(1, n_dp):
            row = (j + k) % n_dp
            rs_arrive(r, row).wait_recv()
            acc = acc + precv[r, row].astype(jnp.float32)
        total = acc[2 * rows:2 * rows + 1] + acc[2 * rows + 1:2 * rows + 2]
        scale = lax.rsqrt(total * (1.0 / (SHIFT * width)) + 1e-05)
        live = scale > 0.0
        arows[r, j, 0] = jnp.where(live, acc[rows:2 * rows] * scale, 0.0).astype(jnp.bfloat16)
        arows[r, j, 1] = jnp.where(live, acc[:rows] * scale, 0.0).astype(jnp.bfloat16)
        for k in range(1, n_dp):
            ag_copy(r, (j + k) % n_dp).start()

    def gradients(r, a):
        mixed = jnp.concatenate([arows[r, row, a] for row in range(n_dp)], axis=1)
        part = lax.dot_general(
            mixed, joined(r, a), (((1,), (1,)), ((), ())), preferred_element_type=jnp.float32
        )
        if r == 0:
            grad[a] = part
        else:
            grad[a] = grad[a] + part

    def first_gradients(r):
        for k in range(1, n_dp):
            ag_arrive(r, (j + k) % n_dp).wait_recv()
        gradients(r, 0)

    def second_gradients(r):
        gradients(r, 1)

    def update():
        for a in range(2):
            factor = -row_factor(a)

            def one(tile, carry):
                here = pl.ds(pl.multiple_of(tile * 128, 128), 128)
                gradient = grad[a, :, here]
                first = m_new[0, a, :, here].astype(jnp.float32)
                second = m_new[1, a, :, here].astype(jnp.float32)
                new_first = beta_one * first + (1.0 - beta_one) * gradient
                new_second = beta_two * second + (1.0 - beta_two) * gradient * gradient
                first_hat = new_first / (1.0 - beta_one**adam_step)
                second_hat = new_second / (1.0 - beta_two**adam_step)
                step = first_hat / (jnp.sqrt(second_hat) + epsilon) + decay * w_new[
                    a, :, here
                ].astype(jnp.float32)
                out_ref[a, :, here] = (factor * step).astype(jnp.bfloat16)
                return carry

            lax.fori_loop(0, cols // 128, one, 0)

    near = (near0, near1, near2)
    far = (far0, far1, far2)
    parts = n_x // 2
    size = rows // parts

    def piece(ref, q):
        return ref.at[q // parts, pl.ds(q % parts * size, size), :]

    def held(ch):
        return w_ref if ch == 0 else short.at[ch - 1]

    def new(ch):
        return w_new if ch == 0 else m_new.at[ch - 1]

    def others(f):
        for k in range(1, n_x):
            f((x + k) % n_x)

    def near_copy(ch, q):
        return to(
            near[ch].at[x], piece(held(ch), q), near_send.at[ch, q], near_recv.at[ch, x],
            pop=side * n_x + q,
        )

    def near_arrive(ch, q):
        here = near[ch].at[q]
        return to(here, here, near_send.at[ch, q], near_recv.at[ch, q], pop=side * n_x + q)

    def far_copy(ch, s):
        return to(
            far[ch].at[s], sent.at[ch, s], far_send.at[ch, s], far_recv.at[ch, s], pop=opposite
        )

    def back_copy(ch, q):
        return to(
            piece(new(ch), x), back.at[ch, q], back_send.at[ch, q], back_recv.at[ch, x],
            pop=side * n_x + q,
        )

    def back_arrive(ch, q):
        here = piece(new(ch), q)
        return to(here, here, back_send.at[ch, q], back_recv.at[ch, q], pop=side * n_x + q)

    def near_out(ch):
        others(lambda q: near_copy(ch, q).start())
        if ch == 0:
            own_weights().start()
        else:
            near[ch][x] = piece(held(ch), x)[...]

    def own_weights():
        return pltpu.make_async_copy(piece(w_ref, x), near[0].at[x], own_sem.at[2])

    def far_out(ch):
        if ch == 0:
            own_weights().wait()
        others(lambda q: near_arrive(ch, q).wait_recv())
        for s in range(n_cross):
            @pl.when(s < n_sent)
            def _():
                sent[ch, s] = near[ch][sends[s]]
                far_copy(ch, s).start()

    def back_out(ch):
        for s in range(n_cross):
            @pl.when(s < n_got)
            def _():
                far_copy(ch, s).wait_recv()

        for q in range(n_x):
            back[ch, q] = near[ch][jnp.minimum(picks[q], n_x - 1)]

        if n_cross:
            @pl.when(n_got > 0)
            def _():
                for q in range(n_x):
                    got = far[ch][jnp.maximum(picks[q] - n_x, 0)]
                    back[ch, q] = jnp.where(picks[q] < n_x, back[ch, q], got)

        others(lambda q: back_copy(ch, q).start())
        piece(new(ch), x)[...] = back[ch, x]

    def back_in(ch):
        others(lambda q: back_arrive(ch, q).wait_recv())

    near_out(0)
    for u in range(2):
        for a, ref in enumerate((act_ref, cot_ref)):
            xt_ref[u, a] = ref[u * HALF:(u + 1) * HALF, :].T
        spread(u)
    for m, wide in enumerate((wide1, wide2)):
        pltpu.make_async_copy(wide, wide, own_sem.at[m]).wait()
        for a in range(2):
            short[m, a] = wide[a].astype(jnp.bfloat16)
        near_out(m + 1)

    whole = rounds * steps * 2
    parts_of = {
        "far": far_out, "back": back_out, "in": back_in,
        "prod": lambda r: (first_products(r), second_products(r)),
        "sum": reduce,
        "grad": lambda r: (first_gradients(r), second_gradients(r)),
    }

    def run(name):
        parts_of[name[:-1]](int(name[-1]))

    during, after = schedule(*counts)

    def turn(f, carry):
        line_step(f // (2 * steps), f // 2 % steps, f % 2)
        for at, names in during:
            @pl.when(f == at * whole // 16)
            def _():
                for name in names:
                    run(name)

        return carry

    lax.fori_loop(0, whole, turn, 0)
    for name in after:
        run(name)
    update()

    def drain(r, carry):
        for k in range(per_row):
            start = j * per_row + k

            @pl.when((start <= c) & (c < chips - 1))
            def _():
                for row in range(n_dp):
                    for a in range(2):
                        go_right(r, k, row, a).wait_send()

            @pl.when((start >= c) & (c > 0))
            def _():
                for row in range(n_dp):
                    for a in range(2):
                        go_left(r, k, row, a).wait_send()

            for row in range(n_dp):
                for a in range(2):
                    pass_sib(r, k, row, a).wait_send()
        for k in range(1, n_dp):
            peer = (j + k) % n_dp
            rs_copy(r, peer).wait_send()
            ag_copy(r, peer).wait_send()

        @pl.when(home != j)
        def _():
            across(r, xt_ref.at[r]).wait_send()

        return carry

    lax.fori_loop(0, rounds, drain, 0)
    for ch in range(3):
        others(lambda q: near_copy(ch, q).wait_send())
        others(lambda q: back_copy(ch, q).wait_send())
        for s in range(n_cross):
            @pl.when(s < n_sent)
            def _():
                far_copy(ch, s).wait_send()


def schedule(there, back):
    if there + back == 0:
        return (
            (
                (2, ("far0", "back0")),
                (6, ("far1", "far2", "back1", "back2")),
                (12, ("in0",)),
                (14, ("prod0",)),
            ),
            ("prod1", "sum0", "sum1", "grad0", "grad1", "in1", "in2"),
        )
    compute = ("prod0", "prod1", "sum0", "sum1")
    if there == back == 1:
        return (
            ((2, ("far0",)), (10, ("back0",))),
            ("far1", "far2", "in0") + compute
            + ("back1", "grad0", "grad1", "back2", "in1", "in2"),
        )
    return (
        ((2, ("far0",)),),
        ("far1", "far2", "back0", "in0") + compute
        + ("grad0", "grad1", "back1", "back2", "in1", "in2"),
    )


def exploit_step(counts, ranking, choice, activations, cotangent, weights, first, second):
    n_pop, n_dp, n_tensor = (lax.axis_size(name) for name in ("pop", "dp", "tensor"))
    rounds = 2
    block = activations.shape[1]
    _, rows, cols = weights.shape
    chips = n_tensor // 2
    per_row = chips // n_dp
    n_x = n_pop // 2
    slots = max(counts + (1,))
    dma = pltpu.SemaphoreType.DMA
    smem = pl.BlockSpec(memory_space=pltpu.SMEM)
    vmem = pl.BlockSpec(memory_space=pltpu.VMEM)
    hbm = pl.BlockSpec(memory_space=pl.ANY)
    bf16 = functools.partial(pltpu.VMEM, dtype=jnp.bfloat16)
    part = (4 * rows // n_pop, cols)
    flops = rounds * 2 * 2 * 2 * rows * cols * n_dp * HALF
    return pl.pallas_call(
        functools.partial(
            kernel, counts, n_pop, n_dp, n_tensor, choice.shape[0] // (2 * n_pop)
        ),
        out_shape=jax.ShapeDtypeStruct((2, rows, cols), jnp.bfloat16),
        in_specs=[smem, smem, vmem, vmem, hbm, hbm, hbm],
        out_specs=vmem,
        scratch_shapes=[
            bf16((rounds, 2, block, HALF)),
            pltpu.VMEM((2, rows, cols), jnp.float32),
            pltpu.VMEM((2, rows, cols), jnp.float32),
        ]
        + [bf16((n_x,) + part)] * 3
        + [bf16((slots,) + part)] * 3
        + [
            bf16((3, slots) + part),
            bf16((3, n_x) + part),
            bf16((2, 2, rows, cols)),
            bf16((2, rows, cols)),
            bf16((2, 2, rows, cols)),
            bf16((rounds, n_dp, 2, cols, HALF)),
            bf16((rounds, n_dp, 2 * rows + 16, HALF)),
            bf16((rounds, n_dp, 2 * rows + 16, HALF)),
            bf16((rounds, n_dp, 2, rows, HALF)),
            pltpu.VMEM((2, rows, cols), jnp.float32),
            dma((rounds,)),
            dma((rounds,)),
            dma((rounds, n_dp)),
            dma((rounds, per_row, n_dp, 2)),
            dma((rounds, per_row, n_dp, 2)),
            dma((rounds, per_row, n_dp, 2)),
            dma((rounds, per_row, n_dp, 2)),
            dma((rounds, per_row, n_dp, 2)),
            dma((rounds, n_dp)),
            dma((rounds, n_dp)),
            dma((rounds, n_dp)),
            dma((rounds, n_dp)),
            dma((3, n_x)),
            dma((3, n_x)),
            dma((3, slots)),
            dma((3, slots)),
            dma((3, n_x)),
            dma((3, n_x)),
            dma((3,)),
        ],
        compiler_params=pltpu.CompilerParams(
            collective_id=crossings(n_x).index(counts), has_side_effects=True, vmem_limit_bytes=56 * 1024 * 1024
        ),
        cost_estimate=pl.CostEstimate(
            flops=flops, bytes_accessed=8 * rows * cols * 4, transcendentals=0
        ),
        name="exploit_%d_%d" % counts,
    )(ranking, choice, activations, cotangent, weights, first, second)


def crossings(n_x):
    return [
        (winners - stay, n_x - winners - stay)
        for winners in range(n_x + 1)
        for stay in range(min(winners, n_x - winners) + 1)
    ]


def per_device(ranking, factor_index, weights, first_moment, second_moment, activations, cotangent):
    n_x = lax.axis_size("pop") // 2
    cases = crossings(n_x)
    winner, loser = ranking[:n_x] // n_x, ranking[n_x:] // n_x
    there, back = jnp.sum(winner < loser), jnp.sum(winner > loser)
    case = sum(
        jnp.where((there == a) & (back == b), n, 0) for n, (a, b) in enumerate(cases)
    ).astype(jnp.int32)
    step = lax.switch(
        case,
        [functools.partial(exploit_step, counts) for counts in cases],
        ranking, factor_index.reshape(-1), activations[0], cotangent[0],
        weights[0], first_moment[0], second_moment[0],
    )
    return step[None]


def solution(mesh):
    in_specs = (
        P(),
        P(),
        P("pop", None, "tensor", "dp"),
        P("pop", None, "tensor", "dp"),
        P("pop", None, "tensor", "dp"),
        P("pop", "dp", "tensor"),
        P("pop", "dp", "tensor"),
    )
    out_specs = P("pop", None, "tensor", "dp")
    return jax.shard_map(
        per_device, mesh=mesh, in_specs=in_specs, out_specs=out_specs, check_vma=False
    )
```

```python
import functools

import jax
import jax.numpy as jnp
from jax import lax
from jax.experimental import pallas as pl
from jax.experimental.pallas import tpu as pltpu
from jax.sharding import PartitionSpec as P

HEAD_SIZE = 128
HALF = 128
SHIFT = 1.0 / 1024.0
CUTS = 4

rate_levels = (0.8, 1.0, 1.25)
beta_one = 0.9
beta_two = 0.95
adam_step = 10
decay = 0.1
epsilon = 1e-08
MESH = pl.DeviceIdType.MESH


def kernel(
    counts, n_pop, n_dp, n_tensor, n_heads,
    rank_ref, choice_ref, act_ref, cot_ref, w_ref, m1_ref, m2_ref,
    out_ref,
    xt_ref, wide1, wide2, near0, near1, near2, far0, far1, far2, sent, back, short, w_new, m_new,
    feat, psend, precv, arows, grad,
    loc_sem, y_send, y_recv, left_sem, right_sem, line_sem, sib_send, sib_recv,
    rs_send, rs_recv, ag_send, ag_recv,
    near_send, near_recv, far_send, far_recv, back_send, back_recv, own_sem,
):
    p = lax.axis_index("pop")
    n_x = n_pop // 2
    side = p // n_x
    x = p % n_x
    opposite = (p + n_x) % n_pop
    n_cross = max(counts)
    n_sent = jnp.where(side == 0, counts[0], counts[1])
    n_got = jnp.where(side == 0, counts[1], counts[0])
    j = lax.axis_index("dp")
    i = lax.axis_index("tensor")
    chips = n_tensor // 2
    c = i // 2
    core = i % 2
    sib = c * 2 + 1 - core
    per_row = chips // n_dp
    rounds = feat.shape[0]
    block = xt_ref.shape[2]
    rows = w_ref.shape[1]
    cols = w_ref.shape[2]
    width = n_dp * cols
    steps = per_row * n_dp
    home = c // per_row
    mine = c % per_row

    for m, (ref, wide) in enumerate(((m1_ref, wide1), (m2_ref, wide2))):
        pltpu.make_async_copy(ref, wide, own_sem.at[m]).start()

    def to(dst, src, send, recv, **where):
        return pltpu.make_async_remote_copy(
            src_ref=src, dst_ref=dst, send_sem=send, recv_sem=recv,
            device_id=where, device_id_type=MESH,
        )

    barrier = pltpu.get_barrier_semaphore()
    pl.semaphore_signal(barrier, inc=1, device_id={"tensor": sib}, device_id_type=MESH)
    for k in range(1, n_dp):
        pl.semaphore_signal(
            barrier, inc=1, device_id={"dp": (j + k) % n_dp}, device_id_type=MESH
        )
    for k in range(1, n_x):
        pl.semaphore_signal(
            barrier, inc=1, device_id={"pop": side * n_x + (x + k) % n_x}, device_id_type=MESH
        )
    pl.semaphore_signal(barrier, inc=1, device_id={"pop": opposite}, device_id_type=MESH)

    @pl.when(c > 0)
    def _():
        pl.semaphore_signal(barrier, inc=1, device_id={"tensor": i - 2}, device_id_type=MESH)

    @pl.when(c < chips - 1)
    def _():
        pl.semaphore_signal(barrier, inc=1, device_id={"tensor": i + 2}, device_id_type=MESH)

    sends = [jnp.int32(0)] * max(n_cross, 1)
    picks = [jnp.int32(q) for q in range(n_x)]
    losing = jnp.int32(0)
    arrived = [jnp.int32(0), jnp.int32(0)]
    for pair in range(n_x):
        winner, loser = rank_ref[pair], rank_ref[n_x + pair]
        w_side, l_side = lax.div(winner, n_x), lax.div(loser, n_x)
        w_x = winner - w_side * n_x
        cross = w_side != l_side
        slot = jnp.where(l_side > 0, arrived[1], arrived[0])
        arrived = [
            arrived[0] + jnp.where(cross & (l_side == 0), 1, 0),
            arrived[1] + jnp.where(cross & (l_side > 0), 1, 0),
        ]
        sends = [
            jnp.where(cross & (w_side == side) & (slot == n), w_x, old)
            for n, old in enumerate(sends)
        ]
        picks = [
            jnp.where(loser == side * n_x + q, jnp.where(cross, n_x + slot, w_x), old)
            for q, old in enumerate(picks)
        ]
        losing = jnp.where(loser == p, 1, losing)

    def levels(a, head):
        choice = choice_ref[p, a, jnp.minimum(head, n_heads - 1)]
        level = jnp.where(
            choice == 0, rate_levels[0], jnp.where(choice == 1, rate_levels[1], rate_levels[2])
        )
        return jnp.where(losing > 0, level, 1.0)

    def row_factor(a):
        first_row = i * rows
        head = first_row // HEAD_SIZE
        at = lax.broadcasted_iota(jnp.int32, (rows, 128), 0) + (first_row - head * HEAD_SIZE)
        return jnp.where(
            at < HEAD_SIZE,
            levels(a, head),
            jnp.where(at < 2 * HEAD_SIZE, levels(a, head + 1), levels(a, head + 2)),
        )

    inner = (c > 0) & (c < chips - 1)

    @pl.when(inner)
    def _():
        pl.semaphore_wait(barrier, n_dp + n_x + 2)

    @pl.when(jnp.logical_not(inner))
    def _():
        pl.semaphore_wait(barrier, n_dp + n_x + 1)

    def place(r, row, k, half):
        return feat.at[r, row, :, pl.ds((k * 2 + half) * block, block), :]

    def keep(r, src):
        return pltpu.make_async_copy(src, place(r, j, mine, core), loc_sem.at[r])

    def across(r, src):
        return to(place(r, j, mine, core), src, y_send.at[r], y_recv.at[r, j], dp=home)

    def arrive(r, row):
        here = place(r, row, mine, core)
        return to(here, here, y_send.at[r], y_recv.at[r, row], dp=row)

    def place_of(r, row, k, half, a):
        cut = block // (CUTS // 2)
        begin = (k * 2 + half) * block + a % (CUTS // 2) * cut
        return feat.at[r, row, a // (CUTS // 2), pl.ds(begin, cut), :]

    def go_right(r, k, row, a):
        here = place_of(r, row, k, core, a)
        at = (r, k, row, a)
        return to(here, here, right_sem.at[at], line_sem.at[at], tensor=i + 2)

    def go_left(r, k, row, a):
        here = place_of(r, row, k, core, a)
        at = (r, k, row, a)
        return to(here, here, left_sem.at[at], line_sem.at[at], tensor=i - 2)

    def pass_sib(r, k, row, a):
        here = place_of(r, row, k, core, a)
        at = (r, k, row, a)
        return to(here, here, sib_send.at[at], sib_recv.at[at], tensor=sib)

    def from_sib(r, k, row, a):
        here = place_of(r, row, k, 1 - core, a)
        at = (r, k, row, a)
        return to(here, here, sib_send.at[at], sib_recv.at[at], tensor=sib)

    def spread(r):
        @pl.when(home == j)
        def _():
            keep(r, xt_ref.at[r]).start()

        @pl.when(home != j)
        def _():
            across(r, xt_ref.at[r]).start()

    def line_step(r, n, a):
        first = jnp.where(c <= j * per_row, 0, 1)
        k = jnp.where(n < n_dp, first, 1 - first)
        row = (j + n) % n_dp
        start = j * per_row + k

        @pl.when((start == c) & (row == j) & (a == 0))
        def _():
            keep(r, place(r, j, mine, core)).wait()

        @pl.when((start == c) & (row != j) & (a == 0))
        def _():
            arrive(r, row).wait_recv()

        @pl.when(start < c)
        def _():
            go_right(r, k, row, a).wait_recv()

        @pl.when(start > c)
        def _():
            go_left(r, k, row, a).wait_recv()

        @pl.when((start <= c) & (c < chips - 1))
        def _():
            go_right(r, k, row, a).start()

        @pl.when((start >= c) & (c > 0))
        def _():
            go_left(r, k, row, a).start()

        pass_sib(r, k, row, a).start()

    def rs_copy(r, peer):
        return to(
            precv.at[r, j], psend.at[r, peer], rs_send.at[r, peer], rs_recv.at[r, j], dp=peer
        )

    def rs_arrive(r, peer):
        return to(
            precv.at[r, peer], psend.at[r, peer], rs_send.at[r, peer], rs_recv.at[r, peer], dp=peer
        )

    def ag_copy(r, peer):
        return to(
            arows.at[r, j], arows.at[r, j], ag_send.at[r, peer], ag_recv.at[r, j], dp=peer
        )

    def ag_arrive(r, peer):
        return to(
            arows.at[r, peer], arows.at[r, peer], ag_send.at[r, peer], ag_recv.at[r, peer], dp=peer
        )

    def joined(r, a):
        return jnp.concatenate([feat[r, row, a] for row in range(n_dp)], axis=1)

    def products(r, a):
        part = jnp.dot(w_new[a], joined(r, a), preferred_element_type=jnp.float32)
        for row in range(n_dp):
            psend[r, row, a * rows:(a + 1) * rows, :] = part[
                :, row * HALF:(row + 1) * HALF
            ].astype(jnp.bfloat16)

    def first_products(r):
        for k in range(per_row):
            for row in range(n_dp):
                for a in range(CUTS):
                    from_sib(r, k, row, a).wait_recv()
        products(r, 0)

    def second_products(r):
        products(r, 1)
        for row in range(n_dp):
            wide = feat[r, row, 0].astype(jnp.float32)
            total = jnp.sum(wide * wide, axis=0, keepdims=True) * SHIFT
            high = total.astype(jnp.bfloat16)
            low = jnp.where(total < 1e37, total - high.astype(jnp.float32), 0.0)
            psend[r, row, 2 * rows:2 * rows + 16, :] = jnp.concatenate(
                [high.astype(jnp.float32), low, jnp.zeros((14, HALF), jnp.float32)], axis=0
            ).astype(jnp.bfloat16)
        for k in range(1, n_dp):
            rs_copy(r, (j + k) % n_dp).start()

    def reduce(r):
        acc = psend[r, j].astype(jnp.float32)
        for k in range(1, n_dp):
            row = (j + k) % n_dp
            rs_arrive(r, row).wait_recv()
            acc = acc + precv[r, row].astype(jnp.float32)
        total = acc[2 * rows:2 * rows + 1] + acc[2 * rows + 1:2 * rows + 2]
        scale = lax.rsqrt(total * (1.0 / (SHIFT * width)) + 1e-05)
        live = scale > 0.0
        arows[r, j, 0] = jnp.where(live, acc[rows:2 * rows] * scale, 0.0).astype(jnp.bfloat16)
        arows[r, j, 1] = jnp.where(live, acc[:rows] * scale, 0.0).astype(jnp.bfloat16)
        for k in range(1, n_dp):
            ag_copy(r, (j + k) % n_dp).start()

    def gradients(r, a):
        mixed = jnp.concatenate([arows[r, row, a] for row in range(n_dp)], axis=1)
        part = lax.dot_general(
            mixed, joined(r, a), (((1,), (1,)), ((), ())), preferred_element_type=jnp.float32
        )
        if r == 0:
            grad[a] = part
        else:
            grad[a] = grad[a] + part

    def first_gradients(r):
        for k in range(1, n_dp):
            ag_arrive(r, (j + k) % n_dp).wait_recv()
        gradients(r, 0)

    def second_gradients(r):
        gradients(r, 1)

    def update():
        for a in range(2):
            factor = -row_factor(a)

            def one(tile, carry):
                here = pl.ds(pl.multiple_of(tile * 128, 128), 128)
                gradient = grad[a, :, here]
                first = m_new[0, a, :, here].astype(jnp.float32)
                second = m_new[1, a, :, here].astype(jnp.float32)
                new_first = beta_one * first + (1.0 - beta_one) * gradient
                new_second = beta_two * second + (1.0 - beta_two) * gradient * gradient
                first_hat = new_first / (1.0 - beta_one**adam_step)
                second_hat = new_second / (1.0 - beta_two**adam_step)
                step = first_hat / (jnp.sqrt(second_hat) + epsilon) + decay * w_new[
                    a, :, here
                ].astype(jnp.float32)
                out_ref[a, :, here] = (factor * step).astype(jnp.bfloat16)
                return carry

            lax.fori_loop(0, cols // 128, one, 0)

    near = (near0, near1, near2)
    far = (far0, far1, far2)
    parts = n_x // 2
    size = rows // parts

    def piece(ref, q):
        return ref.at[q // parts, pl.ds(q % parts * size, size), :]

    def held(ch):
        return w_ref if ch == 0 else short.at[ch - 1]

    def new(ch):
        return w_new if ch == 0 else m_new.at[ch - 1]

    def others(f):
        for k in range(1, n_x):
            f((x + k) % n_x)

    def near_copy(ch, q):
        return to(
            near[ch].at[x], piece(held(ch), q), near_send.at[ch, q], near_recv.at[ch, x],
            pop=side * n_x + q,
        )

    def near_arrive(ch, q):
        here = near[ch].at[q]
        return to(here, here, near_send.at[ch, q], near_recv.at[ch, q], pop=side * n_x + q)

    def far_copy(ch, s):
        return to(
            far[ch].at[s], sent.at[ch, s], far_send.at[ch, s], far_recv.at[ch, s], pop=opposite
        )

    def back_copy(ch, q):
        return to(
            piece(new(ch), x), back.at[ch, q], back_send.at[ch, q], back_recv.at[ch, x],
            pop=side * n_x + q,
        )

    def back_arrive(ch, q):
        here = piece(new(ch), q)
        return to(here, here, back_send.at[ch, q], back_recv.at[ch, q], pop=side * n_x + q)

    def near_out(ch):
        others(lambda q: near_copy(ch, q).start())
        if ch == 0:
            own_weights().start()
        else:
            near[ch][x] = piece(held(ch), x)[...]

    def own_weights():
        return pltpu.make_async_copy(piece(w_ref, x), near[0].at[x], own_sem.at[2])

    def far_out(ch):
        if ch == 0:
            own_weights().wait()
        others(lambda q: near_arrive(ch, q).wait_recv())
        for s in range(n_cross):
            @pl.when(s < n_sent)
            def _():
                sent[ch, s] = near[ch][sends[s]]
                far_copy(ch, s).start()

    def back_out(ch):
        for s in range(n_cross):
            @pl.when(s < n_got)
            def _():
                far_copy(ch, s).wait_recv()

        for q in range(n_x):
            back[ch, q] = near[ch][jnp.minimum(picks[q], n_x - 1)]

        if n_cross:
            @pl.when(n_got > 0)
            def _():
                for q in range(n_x):
                    got = far[ch][jnp.maximum(picks[q] - n_x, 0)]
                    back[ch, q] = jnp.where(picks[q] < n_x, back[ch, q], got)

        others(lambda q: back_copy(ch, q).start())
        piece(new(ch), x)[...] = back[ch, x]

    def back_in(ch):
        others(lambda q: back_arrive(ch, q).wait_recv())

    near_out(0)
    for u in range(2):
        for a, ref in enumerate((act_ref, cot_ref)):
            xt_ref[u, a] = ref[:, u * HALF:(u + 1) * HALF]
        spread(u)
    for m, wide in enumerate((wide1, wide2)):
        pltpu.make_async_copy(wide, wide, own_sem.at[m]).wait()
        for a in range(2):
            short[m, a] = wide[a].astype(jnp.bfloat16)
        near_out(m + 1)

    whole = rounds * steps * CUTS
    parts_of = {
        "far": far_out, "back": back_out, "in": back_in,
        "prod": lambda r: (first_products(r), second_products(r)),
        "sum": reduce,
        "grad": lambda r: (first_gradients(r), second_gradients(r)),
    }

    def run(name):
        parts_of[name[:-1]](int(name[-1]))

    during, after = schedule(*counts)

    def turn(f, carry):
        line_step(f // (CUTS * steps), f // CUTS % steps, f % CUTS)
        for at, names in during:
            @pl.when(f == at * whole // 16)
            def _():
                for name in names:
                    run(name)

        return carry

    lax.fori_loop(0, whole, turn, 0)
    for name in after:
        run(name)
    update()

    def drain(r, carry):
        for k in range(per_row):
            start = j * per_row + k

            @pl.when((start <= c) & (c < chips - 1))
            def _():
                for row in range(n_dp):
                    for a in range(CUTS):
                        go_right(r, k, row, a).wait_send()

            @pl.when((start >= c) & (c > 0))
            def _():
                for row in range(n_dp):
                    for a in range(CUTS):
                        go_left(r, k, row, a).wait_send()

            for row in range(n_dp):
                for a in range(CUTS):
                    pass_sib(r, k, row, a).wait_send()
        for k in range(1, n_dp):
            peer = (j + k) % n_dp
            rs_copy(r, peer).wait_send()
            ag_copy(r, peer).wait_send()

        @pl.when(home != j)
        def _():
            across(r, xt_ref.at[r]).wait_send()

        return carry

    lax.fori_loop(0, rounds, drain, 0)
    for ch in range(3):
        others(lambda q: near_copy(ch, q).wait_send())
        others(lambda q: back_copy(ch, q).wait_send())
        for s in range(n_cross):
            @pl.when(s < n_sent)
            def _():
                far_copy(ch, s).wait_send()


def schedule(there, back):
    if there + back == 0:
        return (
            (
                (2, ("far0", "back0")),
                (6, ("far1", "far2", "back1", "back2")),
                (12, ("in0",)),
                (14, ("prod0",)),
            ),
            ("prod1", "sum0", "sum1", "grad0", "grad1", "in1", "in2"),
        )
    compute = ("prod0", "prod1", "sum0", "sum1")
    if there == back == 1:
        return (
            ((2, ("far0",)), (10, ("back0",))),
            ("far1", "far2", "in0") + compute
            + ("back1", "grad0", "grad1", "back2", "in1", "in2"),
        )
    return (
        ((2, ("far0",)),),
        ("far1", "far2", "back0", "in0") + compute
        + ("grad0", "grad1", "back1", "back2", "in1", "in2"),
    )


def exploit_step(counts, ranking, choice, activations, cotangent, weights, first, second):
    n_pop, n_dp, n_tensor = (lax.axis_size(name) for name in ("pop", "dp", "tensor"))
    rounds = 2
    block = activations.shape[0]
    _, rows, cols = weights.shape
    chips = n_tensor // 2
    per_row = chips // n_dp
    n_x = n_pop // 2
    slots = max(counts + (1,))
    dma = pltpu.SemaphoreType.DMA
    smem = pl.BlockSpec(memory_space=pltpu.SMEM)
    vmem = pl.BlockSpec(memory_space=pltpu.VMEM)
    hbm = pl.BlockSpec(memory_space=pl.ANY)
    bf16 = functools.partial(pltpu.VMEM, dtype=jnp.bfloat16)
    part = (4 * rows // n_pop, cols)
    flops = rounds * 2 * 2 * 2 * rows * cols * n_dp * HALF
    return pl.pallas_call(
        functools.partial(
            kernel, counts, n_pop, n_dp, n_tensor, choice.shape[2]
        ),
        out_shape=jax.ShapeDtypeStruct((2, rows, cols), jnp.bfloat16),
        in_specs=[smem, smem, vmem, vmem, hbm, hbm, hbm],
        out_specs=vmem,
        scratch_shapes=[
            bf16((rounds, 2, block, HALF)),
            pltpu.VMEM((2, rows, cols), jnp.float32),
            pltpu.VMEM((2, rows, cols), jnp.float32),
        ]
        + [bf16((n_x,) + part)] * 3
        + [bf16((slots,) + part)] * 3
        + [
            bf16((3, slots) + part),
            bf16((3, n_x) + part),
            bf16((2, 2, rows, cols)),
            bf16((2, rows, cols)),
            bf16((2, 2, rows, cols)),
            bf16((rounds, n_dp, 2, cols, HALF)),
            bf16((rounds, n_dp, 2 * rows + 16, HALF)),
            bf16((rounds, n_dp, 2 * rows + 16, HALF)),
            bf16((rounds, n_dp, 2, rows, HALF)),
            pltpu.VMEM((2, rows, cols), jnp.float32),
            dma((rounds,)),
            dma((rounds,)),
            dma((rounds, n_dp)),
            dma((rounds, per_row, n_dp, CUTS)),
            dma((rounds, per_row, n_dp, CUTS)),
            dma((rounds, per_row, n_dp, CUTS)),
            dma((rounds, per_row, n_dp, CUTS)),
            dma((rounds, per_row, n_dp, CUTS)),
            dma((rounds, n_dp)),
            dma((rounds, n_dp)),
            dma((rounds, n_dp)),
            dma((rounds, n_dp)),
            dma((3, n_x)),
            dma((3, n_x)),
            dma((3, slots)),
            dma((3, slots)),
            dma((3, n_x)),
            dma((3, n_x)),
            dma((3,)),
        ],
        compiler_params=pltpu.CompilerParams(
            collective_id=crossings(n_x).index(counts), has_side_effects=True, vmem_limit_bytes=56 * 1024 * 1024
        ),
        cost_estimate=pl.CostEstimate(
            flops=flops, bytes_accessed=8 * rows * cols * 4, transcendentals=0
        ),
        name="exploit_%d_%d" % counts,
    )(ranking, choice, activations, cotangent, weights, first, second)


def crossings(n_x):
    return [
        (winners - stay, n_x - winners - stay)
        for winners in range(n_x + 1)
        for stay in range(min(winners, n_x - winners) + 1)
    ]


def per_device(ranking, factor_index, weights, first_moment, second_moment, activations, cotangent):
    n_x = lax.axis_size("pop") // 2
    cases = crossings(n_x)
    winner, loser = ranking[:n_x] // n_x, ranking[n_x:] // n_x
    crossed = jnp.sum(
        jnp.where(winner < loser, 1, 0) + jnp.where(winner > loser, n_x + 1, 0)
    )
    codes = jnp.array([a + (n_x + 1) * b for a, b in cases], jnp.int32)
    case = jnp.sum(jnp.where(codes == crossed, jnp.arange(len(cases)), 0)).astype(jnp.int32)
    step = lax.switch(
        case,
        [functools.partial(exploit_step, counts) for counts in cases],
        ranking, factor_index, activations[0].T, cotangent[0].T,
        weights[0], first_moment[0], second_moment[0],
    )
    return step[None]


def solution(mesh):
    in_specs = (
        P(),
        P(),
        P("pop", None, "tensor", "dp"),
        P("pop", None, "tensor", "dp"),
        P("pop", None, "tensor", "dp"),
        P("pop", "dp", "tensor"),
        P("pop", "dp", "tensor"),
    )
    out_specs = P("pop", None, "tensor", "dp")
    return jax.shard_map(
        per_device, mesh=mesh, in_specs=in_specs, out_specs=out_specs, check_vma=False
    )
```
